32 devices in a mesh: groups: 2 (over y), hidden: 8 (over z, core), mp: 2 (over x).
Axes of the slice: x: 2, y: 2, z: 4, core: 2. Of those that a mesh axis runs over, the one named last changes fastest.
Arguments:
- stream_rows: bfloat16 [64, 2, 16384], P(('groups', 'hidden'), None, 'mp'), parts along dimension 0, may hold values from -6 to 6
- norm_gain: bfloat16 [16384], P('mp'), may hold values from 0.5 to 1.5
- query_weight: bfloat16 [16384, 8, 1024], P('hidden', 'mp'), may hold values from -0.046875 to 0.046875
- keyval_weight: bfloat16 [16384, 8, 256], P('hidden', 'mp'), may hold values from -0.046875 to 0.046875
- output_weight: bfloat16 [8, 1024, 16384], P('mp', None, 'hidden'), may hold values from -0.25 to 0.25
- key_cache: bfloat16 [64, 8, 1024, 128], P(('groups', 'hidden'), 'mp'), parts along dimension 0, may hold values from -400 to 400
- value_cache: bfloat16 [64, 8, 1024, 128], P(('groups', 'hidden'), 'mp'), parts along dimension 0, may hold values from -6 to 6
- lengths: int32 [64], P(('groups', 'hidden')), parts along dimension 0, may hold values from 128 to 1024, as said below
Outputs:
- branch: bfloat16 [64, 2, 16384], P(('groups', 'mp'), None, 'hidden'), parts along dimension 0
The draws below stay inside these ranges and needn't reach their ends.
There are 2 independent parts, one for each index of `groups`. The reference program is written for one: setup_inputs(seed, part) draws one part's arguments, and reference() takes and returns one part's arrays. A program takes and returns all parts, laid end to end along the dimension named above; an argument that names none is the same for every part. Nothing has to cross between parts.
Inputs may be any that keep to these rules, and one draw needn't show every extreme that they name: `lengths`: in each group, one sequence has exactly 1024 filled slots and one exactly 128.
All inputs are finite; a program needn't handle non-finite values.
Results may differ from the reference program's by a relative error of at most 0.0055.
The reference program's roundings to bfloat16 on the way count: a program that leaves them out, or rounds other values in their place, can miss the bound.
Values may be sent and summed in bfloat16 or wider, within the bound.
A program may use at most 192 MiB of HBM per device.

```python
import math
import jax
import jax.numpy as jnp
from jax import lax

D = 16384
QHEADS = 64
KVHEADS = 8
HEAD = 128
QPER = 8
CACHE = 1024
STEPS = 2
BATCH = 32


def draw_lengths(key, part):
    key = jax.random.fold_in(key, 11)
    first, second = jax.random.split(key)
    base = jax.random.randint(first, (BATCH,), CACHE // 8, CACHE + 1, dtype=jnp.int32)
    order = jax.random.permutation(second, BATCH)
    base = base.at[order[0]].set(CACHE)
    base = base.at[order[1]].set(CACHE // 8)
    return base.astype(jnp.int32)


def draw_key_cache(key, part):
    key = jax.random.fold_in(key, 23)
    first = jax.random.fold_in(key, 0)
    shape = (BATCH, KVHEADS, CACHE, HEAD)
    values = jnp.clip(jax.random.normal(first, shape, jnp.float32) * 1.5, -9.0, 9.0)
    return values.astype(jnp.bfloat16)


def block_levels(key, shape, shards, least, high):
    loudness = 1.0
    for dim, shards_of in shards:
        steps = jax.random.uniform(jax.random.fold_in(jax.random.fold_in(key, 6), dim), (shards_of,), jnp.float32, least / len(shards), high / len(shards))
        loudness = loudness * jnp.repeat(jnp.exp(steps), shape[dim] // shards_of).reshape((-1,) + (1,) * (len(shape) - 1 - dim))
    return loudness


def bell_draw(own_key, extent, width, limit, cuts=(), held_as=jnp.bfloat16):
    result = jax.random.normal(own_key, extent, jnp.float32) * width
    if len(cuts) > 0:
        result = block_levels(own_key, extent, cuts, -0.22, 0.18) * result
    return jnp.clip(result, min=-limit, max=limit).astype(held_as)


def setup_inputs(seed: int = 0, part: int = 0) -> dict:
    key_list = jax.random.split(jax.random.key(seed), 9)
    own_keys = jax.random.split(jax.random.fold_in(key_list[8], part), 9)
    return {
        "stream_rows": bell_draw(own_keys[0], (BATCH, STEPS, D), 1.0, 6.0, ((0, 8), (2, 2))),
        "norm_gain": jnp.clip(1.0 + 0.1 * jax.random.normal(key_list[1], (D,), jnp.float32), 0.5, 1.5).astype(jnp.bfloat16),
        "query_weight": bell_draw(key_list[2], (D, KVHEADS, QPER * HEAD), D ** -0.5, 0.046875, ((0, 8), (1, 2))),
        "keyval_weight": bell_draw(key_list[3], (D, KVHEADS, 2 * HEAD), D ** -0.5, 0.046875, ((0, 8), (1, 2))),
        "output_weight": bell_draw(key_list[4], (KVHEADS, QPER * HEAD, D), (QHEADS * HEAD // 16) ** -0.5, 0.25, ((0, 2), (2, 8))),
        "key_cache": draw_key_cache(jax.random.fold_in(jax.random.fold_in(key_list[8], part), 71), part),
        "value_cache": bell_draw(own_keys[6], (BATCH, KVHEADS, CACHE, HEAD), 1.0, 6.0, ((0, 8), (1, 2))),
        "lengths": draw_lengths(jax.random.fold_in(jax.random.fold_in(key_list[8], part), 71), part),
    }


rope_base = 500000.0

def norm_rows(rows, gains):
    values = rows.astype(jnp.float32)
    scale = lax.rsqrt(lax.optimization_barrier(jnp.mean(values * values, axis=-1, keepdims=True)) + 1e-05)
    return (values * scale * gains.astype(jnp.float32)).astype(jnp.bfloat16)

def rotate(values, pos):
    half = values.shape[-1] // 2
    freq = jnp.exp(jnp.arange(half, dtype=jnp.float32) * (-2.0 * math.log(rope_base) / values.shape[-1]))
    angle = pos[..., None] * freq
    cosine = jnp.cos(angle)
    sine = jnp.sin(angle)
    first = values[..., :half]
    second = values[..., half:]
    return jnp.concatenate([first * cosine - second * sine, second * cosine + first * sine], axis=-1)

def attend_one(args):
    query, new_keys, new_vals, keys, vals, length = args
    scale = HEAD ** (-0.5)
    slots = jnp.arange(CACHE) < length
    outs = []
    for step in range(STEPS):
        qf = query[step].astype(jnp.float32)
        cached = jnp.einsum('gqd,gkd->gqk', qf, keys.astype(jnp.float32)) * scale
        fresh = jnp.einsum('gqd,tgd->gqt', qf, new_keys.astype(jnp.float32)) * scale
        keep = jnp.arange(STEPS) <= step
        cached = jnp.where(slots, cached, -jnp.inf)
        fresh = jnp.where(keep, fresh, -jnp.inf)
        top = jnp.maximum(lax.optimization_barrier(jnp.max(cached, axis=-1)), lax.optimization_barrier(jnp.max(fresh, axis=-1)))[..., None]
        p_cached = jnp.where(slots, jnp.exp(cached - top), 0.0)
        p_fresh = jnp.where(keep, jnp.exp(fresh - top), 0.0)
        total = lax.optimization_barrier(jnp.sum(p_cached, axis=-1)) + lax.optimization_barrier(jnp.sum(p_fresh, axis=-1))
        acc = jnp.einsum('gqk,gkd->gqd', p_cached.astype(jnp.bfloat16).astype(jnp.float32), vals.astype(jnp.float32))
        acc = acc + jnp.einsum('gqt,tgd->gqd', p_fresh.astype(jnp.bfloat16).astype(jnp.float32), new_vals.astype(jnp.float32))
        outs.append((acc / total[..., None]).astype(jnp.bfloat16))
    return jnp.stack(outs, axis=0)

def reference(stream_rows, norm_gain, query_weight, keyval_weight, output_weight, key_cache, value_cache, lengths):
    normed = norm_rows(stream_rows, norm_gain).reshape(BATCH * STEPS, D)
    qraw = jnp.dot(normed, query_weight.reshape(D, KVHEADS * QPER * HEAD), preferred_element_type=jnp.float32)
    kvraw = jnp.dot(normed, keyval_weight.reshape(D, KVHEADS * 2 * HEAD), preferred_element_type=jnp.float32)
    qraw = qraw.reshape(BATCH, STEPS, KVHEADS, QPER, HEAD)
    kvraw = kvraw.reshape(BATCH, STEPS, KVHEADS, 2, HEAD)
    pos = (lengths[:, None] + jnp.arange(STEPS, dtype=jnp.int32)[None, :]).astype(jnp.float32)
    query = rotate(qraw, pos[:, :, None, None]).astype(jnp.bfloat16)
    new_keys = rotate(kvraw[:, :, :, 0, :], pos[:, :, None]).astype(jnp.bfloat16)
    new_vals = kvraw[:, :, :, 1, :].astype(jnp.bfloat16)
    heads = lax.map(attend_one, (query, new_keys, new_vals, key_cache, value_cache, lengths))
    heads = heads.reshape(BATCH * STEPS, KVHEADS * QPER * HEAD)
    branch = jnp.dot(heads, output_weight.reshape(KVHEADS * QPER * HEAD, D), preferred_element_type=jnp.float32)
    return branch.reshape(BATCH, STEPS, D).astype(jnp.bfloat16)
```

```python
import functools
import math

import jax
import jax.numpy as jnp
from jax import lax
from jax.experimental import pallas as pl
from jax.experimental.pallas import tpu as pltpu
from jax.sharding import PartitionSpec as P

rope_base = 500000.0


def norm_blocks(pieces, gains, blocks):
    values = pieces.astype(jnp.float32)
    scale = lax.rsqrt(jnp.mean(values * values, axis=(0, 3), keepdims=True) + 1e-05)
    scaled = values * scale * gains.astype(jnp.float32)[:, None, None, :]
    width_parts, seqs, steps_all, narrow = scaled.shape
    whole = jnp.transpose(scaled, (1, 2, 0, 3)).reshape(
        seqs, steps_all, blocks, width_parts * narrow // blocks
    )
    return jnp.transpose(whole, (2, 0, 1, 3)).astype(jnp.bfloat16)


def rotate(values, pos):
    half = values.shape[-1] // 2
    freq = jnp.exp(
        jnp.arange(half, dtype=jnp.float32) * (-2.0 * math.log(rope_base) / values.shape[-1])
    )
    angle = pos[..., None] * freq
    cosine = jnp.cos(angle)
    sine = jnp.sin(angle)
    first = values[..., :half]
    second = values[..., half:]
    return jnp.concatenate(
        [first * cosine - second * sine, second * cosine + first * sine], axis=-1
    )


def attend(query, new_keys, new_vals, key_cache, value_cache, lengths, step, width, count):
    scale = query.shape[-1] ** (-0.5)
    fresh = (
        jnp.einsum("sgqd,stgd->sgqt", query, new_keys, preferred_element_type=jnp.float32) * scale
    )
    keep = jnp.arange(new_keys.shape[1]) <= step
    fresh = jnp.where(keep, fresh, -jnp.inf)

    def block_scores(index):
        scores = (
            jnp.einsum("sgqd,sgkd->sgqk", query, key_cache, preferred_element_type=jnp.float32)
            * scale
        )
        slots = (index * width + jnp.arange(width))[None, :] < lengths[:, None]
        return (scores, slots[:, None, None, :])

    def widen(index, top):
        scores, slots = block_scores(index)
        return jnp.maximum(top, jnp.max(jnp.where(slots, scores, -jnp.inf), axis=-1))

    top = lax.fori_loop(0, count, widen, jnp.max(fresh, axis=-1))
    p_fresh = jnp.where(keep, jnp.exp(fresh - top[..., None]), 0.0)
    total = jnp.sum(p_fresh, axis=-1)
    acc = jnp.einsum(
        "sgqt,stgd->sgqd",
        p_fresh.astype(jnp.bfloat16),
        new_vals,
        preferred_element_type=jnp.float32,
    )

    def accumulate(index, carry):
        acc_now, total_now = carry
        scores, slots = block_scores(index)
        weights = jnp.where(slots, jnp.exp(scores - top[..., None]), 0.0)
        acc_now = acc_now + jnp.einsum(
            "sgqk,sgkd->sgqd",
            weights.astype(jnp.bfloat16),
            value_cache,
            preferred_element_type=jnp.float32,
        )
        return (acc_now, total_now + jnp.sum(weights, axis=-1))

    acc, total = lax.fori_loop(0, count, accumulate, (acc, total))
    return (acc / total[..., None]).astype(jnp.bfloat16)


def local(
    stream_rows,
    norm_gain,
    query_weight,
    keyval_weight,
    output_weight,
    key_cache,
    value_cache,
    lengths,
):
    seqs = stream_rows.shape[0]
    steps_all = stream_rows.shape[1]
    narrow = stream_rows.shape[2]
    pieces, gains = (
        lax.all_gather(stream_rows.reshape(1, seqs, steps_all, narrow), "mp", axis=0, tiled=True),
        lax.all_gather(norm_gain.reshape(1, narrow), "mp", axis=0, tiled=True),
    )
    blocks = lax.axis_size("hidden")
    normed = norm_blocks(pieces, gains, blocks)
    block = query_weight.shape[0]
    groups_here = query_weight.shape[1]
    head = keyval_weight.shape[2] // 2
    per_group = query_weight.shape[2] // head
    q_cols = groups_here * per_group * head
    wq_flat = query_weight.reshape(block, q_cols)
    wkv_flat = keyval_weight.reshape(block, groups_here * 2 * head)
    wo_flat = output_weight.reshape(q_cols, output_weight.shape[2])
    spread = lax.all_to_all(normed, "hidden", split_axis=0, concat_axis=0, tiled=True)
    spread = spread.reshape(blocks * seqs, steps_all, block)
    piece = spread
    flat = piece.reshape(-1, block)
    q_part = jnp.dot(flat, wq_flat, preferred_element_type=jnp.float32)
    kv_part = jnp.dot(flat, wkv_flat, preferred_element_type=jnp.float32)
    joined = jnp.concatenate([q_part, kv_part], axis=1)
    sums = lax.psum_scatter(
        joined.reshape(piece.shape[:-1] + (joined.shape[-1],)),
        "hidden",
        scatter_dimension=0,
        tiled=True,
    )
    qraw = sums[..., :q_cols].reshape(seqs, steps_all, groups_here, per_group, head)
    kvraw = sums[..., q_cols:].reshape(seqs, steps_all, groups_here, 2, head)
    pos = (lengths[:, None] + jnp.arange(steps_all, dtype=jnp.int32)[None, :]).astype(jnp.float32)
    query = rotate(qraw, pos[:, :, None, None]).astype(jnp.bfloat16)
    new_keys = rotate(kvraw[:, :, :, 0, :], pos[:, :, None]).astype(jnp.bfloat16)
    new_vals = kvraw[:, :, :, 1, :].astype(jnp.bfloat16)
    slots_all = key_cache.shape[2]
    count = 1
    results = []
    for step in range(steps_all):
        heads = attend(
            query[:, step],
            new_keys,
            new_vals,
            key_cache,
            value_cache,
            lengths,
            step,
            slots_all,
            count,
        )
        results.append(heads.reshape(seqs, q_cols))
    heads_all = jnp.stack(results, axis=1)
    piece = lax.all_gather(heads_all, "hidden", axis=0, tiled=True)
    flat = piece.reshape(-1, q_cols)
    product = jnp.dot(flat, wo_flat, preferred_element_type=jnp.float32)
    partial_value = product.reshape(piece.shape[:-1] + (wo_flat.shape[1],))
    return lax.psum_scatter(partial_value, "mp", scatter_dimension=0, tiled=True).astype(
        jnp.bfloat16
    )


def fused_kernel(
    xb, gain, trig, lens, wq, wkv, wo, kcache, vcache, out,
    xr, ssl, ssr, gbuf, xexp, wbuf, kbuf, vbuf, obuf_w, part, recv1, recv2, hbuf, acc, osend, orecv,
    xsend_sem, xsem, ss_send, ss_sem, gsem, wsem, csem, wosem,
    s1_send, s1_sem, s2_send, s2_sem, h_send, h_sem, f_send, f_sem, o_send, o_sem,
    *, hidden, mp, width,
):
    gy = lax.axis_index("groups")
    h = lax.axis_index("hidden")
    m = lax.axis_index("mp")
    z = h // 2
    c = h % 2
    zs = hidden // 2
    nb, rows, block = xb.shape
    heads_here = wq.shape[1]
    head = kcache.shape[3]
    qper = wq.shape[2] // head
    slots = kcache.shape[2]
    chunks = (qper + 2) // 2
    all_rows = hidden * rows
    depth = block * heads_here

    def at(hh, mm):
        return (gy, hh, mm)

    def remote(src, dst, send, recv, hh, mm):
        return pltpu.make_async_remote_copy(
            src_ref=src, dst_ref=dst, send_sem=send, recv_sem=recv,
            device_id=at(hh, mm), device_id_type=pl.DeviceIdType.MESH,
        )

    def arrived(ref, sem):
        pltpu.make_async_copy(ref, ref, sem).wait()

    weight_copies = []
    for j in range(qper + 2):
        if j < 2:
            src = wkv.at[:, :, pl.ds(j * head, head)]
        else:
            src = wq.at[:, :, pl.ds((j - 2) * head, head)]
        copy = pltpu.make_async_copy(src, wbuf.at[j], wsem.at[j])
        copy.start()
        weight_copies.append(copy)

    barrier = pltpu.get_barrier_semaphore()
    for dh in range(hidden):
        for dm in range(mp):
            if dh or dm:
                pl.semaphore_signal(
                    barrier, inc=1, device_id=at((h + dh) % hidden, (m + dm) % mp),
                    device_id_type=pl.DeviceIdType.MESH,
                )
    pl.semaphore_wait(barrier, hidden * mp - 1)

    row_sends = []
    for b in range(nb):
        for dm in range(mp):
            hh = m * nb + b
            mm = (m + dm) % mp
            copy = remote(
                xb.at[b], xr.at[h], xsend_sem.at[b * mp + dm], xsem.at[h], hh, mm
            )
            if dm == 0:
                mine = hh == h
                local_copy = pltpu.make_async_copy(xb.at[b], xr.at[h], xsem.at[h])

                @pl.when(mine)
                def _(local_copy=local_copy):
                    local_copy.start()

                @pl.when(jnp.logical_not(mine))
                def _(copy=copy):
                    copy.start()

                row_sends.append((copy, mine))
            else:
                copy.start()
                row_sends.append((copy, None))

    holder = h // nb == m
    gain_copy = remote(gain.at[h % nb], gbuf, gsem.at[0], gsem.at[1], h, (m + 1) % mp)
    gain_local = pltpu.make_async_copy(gain.at[h % nb], gbuf, gsem.at[2])

    @pl.when(holder)
    def _():
        gain_copy.start()
        gain_local.start()

    values = xb[...].astype(jnp.float32)
    squares = jnp.sum(jnp.sum(values * values, axis=0), axis=-1, keepdims=True)
    ssl[...] = jnp.broadcast_to(squares, ssl.shape)
    ssr[m, h] = ssl[...]
    ss_sends = []
    for dh in range(hidden):
        for dm in range(mp):
            if dh or dm:
                copy = remote(
                    ssl, ssr.at[m, h], ss_send.at[dh * mp + dm], ss_sem.at[m, h],
                    (h + dh) % hidden, (m + dm) % mp,
                )
                copy.start()
                ss_sends.append(copy)

    cache_copies = []
    for g in range(heads_here):
        pair = (
            pltpu.make_async_copy(kcache.at[:, g], kbuf.at[:, g], csem.at[0, g]),
            pltpu.make_async_copy(vcache.at[:, g], vbuf.at[:, g], csem.at[1, g]),
        )
        for copy in pair:
            copy.start()
        cache_copies.append(pair)
    out_copies = []
    for g in range(heads_here):
        copy = pltpu.make_async_copy(wo.at[g], obuf_w.at[g], wosem.at[g])
        copy.start()
        out_copies.append(copy)

    for dh in range(hidden):
        for dm in range(mp):
            if dh or dm:
                hh = (h + dh) % hidden
                mm = (m + dm) % mp
                arrived(ssr.at[mm, hh], ss_sem.at[mm, hh])

    @pl.when(holder)
    def _():
        gain_local.wait()
        gain_copy.wait_send()

    @pl.when(jnp.logical_not(holder))
    def _():
        gain_copy.wait_recv()

    for src in range(hidden):
        arrived(xr.at[src], xsem.at[src])
    total_sq = jnp.sum(ssr[...], axis=0).reshape(all_rows, ssl.shape[1])
    scale = lax.rsqrt(total_sq / (nb * mp * block) + 1e-05)[:, :1]
    rows_f = xr[...].astype(jnp.float32).reshape(all_rows, block)
    normed = (rows_f * scale * gbuf[...]).astype(jnp.bfloat16)

    lane = 128
    wide = lane * heads_here
    row_of = lax.broadcasted_iota(jnp.int32, (lane, wide), 0)
    col_of = lax.broadcasted_iota(jnp.int32, (lane, wide), 1)
    spread = jnp.where(col_of // heads_here == row_of, 1.0, 0.0).astype(jnp.bfloat16)
    which = lax.broadcasted_iota(jnp.int32, (all_rows, wide), 1) % heads_here
    for i in range(block // lane):
        rep = jnp.dot(
            normed[:, i * lane:(i + 1) * lane], spread, preferred_element_type=jnp.float32
        )
        for g in range(heads_here):
            xexp[g * all_rows:(g + 1) * all_rows, i * wide:(i + 1) * wide] = jnp.where(
                which == g, rep, 0.0
            ).astype(jnp.bfloat16)

    flat_w = wbuf.reshape(qper + 2, depth, head)
    span = min(depth, 2048)
    stage1 = []
    stage2 = []

    def project(ch):
        for j in (2 * ch, 2 * ch + 1):
            weight_copies[j].wait()

        def body(k, total):
            cut = pl.ds(pl.multiple_of(k * span, span), span)
            rhs = jnp.concatenate([flat_w[2 * ch, cut, :], flat_w[2 * ch + 1, cut, :]], axis=1)
            return total + jnp.dot(xexp[:, cut], rhs, preferred_element_type=jnp.float32)

        result = lax.fori_loop(
            0, depth // span, body,
            jnp.zeros((heads_here * all_rows, 2 * head), jnp.float32),
        )
        for g in range(heads_here):
            for hh in range(hidden):
                first = g * all_rows + hh * rows
                part[ch, hh % 2, hh // 2, g] = result[first:first + rows, :]
        copy = remote(
            part.at[ch, 1 - c], recv1.at[ch], s1_send.at[ch], s1_sem.at[ch], z * 2 + 1 - c, m
        )
        copy.start()
        stage1.append(copy)

    def pass_on(ch):
        stage1[ch].wait_recv()
        part[ch, c] = part[ch, c] + recv1[ch]
        for dz in range(1, zs):
            zz = (z + dz) % zs
            copy = remote(
                part.at[ch, c, zz], recv2.at[ch, dz - 1],
                s2_send.at[ch, dz - 1], s2_sem.at[ch, dz - 1], zz * 2 + c, m,
            )
            copy.start()
            stage2.append(copy)

    for ch in range(chunks):
        project(ch)
        if ch:
            pass_on(ch - 1)
    pass_on(chunks - 1)

    cosine = trig[0]
    sine = trig[1]

    def rotated(values):
        return values * cosine + pltpu.roll(values, head // 2, 1) * sine

    for copy in stage2:
        copy.wait_recv()

    def summed(ch, g):
        total = part[ch, c, z, g]
        for dz in range(1, zs):
            total = total + recv2[ch, dz - 1, g]
        return total

    seqs = kcache.shape[0]
    steps = rows // seqs
    many = qper * rows
    row_id = lax.broadcasted_iota(jnp.int32, (many, 1), 0) % rows
    row_seq = row_id // steps
    row_step = row_id % steps
    limit = jnp.concatenate([lens[...]] * qper, axis=0)[:, :1]
    slot_ok = lax.broadcasted_iota(jnp.int32, (many, slots), 1) < limit
    extra = lax.broadcasted_iota(jnp.int32, (many, head), 1)
    fresh_ok = (extra // steps == row_seq) & (extra % steps <= row_step)
    factor = head ** (-0.5)
    rest = jnp.zeros((head - rows, head), jnp.float32)
    nt = (((1,), (1,)), ((), ()))
    head_sends = []
    forwards = []

    def attention(g):
        kv = summed(0, g)
        new_key = jnp.concatenate([rotated(kv[:, :head]), rest], axis=0).astype(jnp.bfloat16)
        new_val = jnp.concatenate([kv[:, head:], rest], axis=0).astype(jnp.bfloat16)
        queries = []
        for ch in range(1, chunks):
            both = summed(ch, g)
            queries.append(rotated(both[:, :head]))
            queries.append(rotated(both[:, head:]))
        query = jnp.concatenate(queries, axis=0).astype(jnp.bfloat16)
        for copy in cache_copies[g]:
            copy.wait()
        scores = None
        for s in range(seqs):
            one = lax.dot_general(query, kbuf[s, g], nt, preferred_element_type=jnp.float32)
            scores = one if s == 0 else jnp.where(row_seq == s, one, scores)
        scores = jnp.where(slot_ok, scores * factor, -jnp.inf)
        fresh = lax.dot_general(query, new_key, nt, preferred_element_type=jnp.float32)
        fresh = jnp.where(fresh_ok, fresh * factor, -jnp.inf)
        top = jnp.maximum(
            jnp.max(scores, axis=-1, keepdims=True), jnp.max(fresh, axis=-1, keepdims=True)
        )
        p = jnp.exp(scores - top)
        p_fresh = jnp.exp(fresh - top)
        total = jnp.sum(p, axis=-1, keepdims=True) + jnp.sum(p_fresh, axis=-1, keepdims=True)
        weights = p.astype(jnp.bfloat16)
        value = None
        for s in range(seqs):
            one = jnp.dot(weights, vbuf[s, g], preferred_element_type=jnp.float32)
            value = one if s == 0 else jnp.where(row_seq == s, one, value)
        value = value + jnp.dot(
            p_fresh.astype(jnp.bfloat16), new_val, preferred_element_type=jnp.float32
        )
        value = value / total
        line = jnp.concatenate([value[j * rows:(j + 1) * rows] for j in range(qper)], axis=1)
        hbuf[g, c, z] = line.astype(jnp.bfloat16)
        sends = []
        for dz in range(1, zs):
            zz = (z + dz) % zs
            copy = remote(
                hbuf.at[g, c, z], hbuf.at[g, c, z],
                h_send.at[g, dz - 1], h_sem.at[g, z], zz * 2 + c, m,
            )
            copy.start()
            sends.append(copy)
        head_sends.append(sends)

    def forward(g):
        for dz in range(1, zs):
            zz = (z + dz) % zs
            arrived(hbuf.at[g, c, zz], h_sem.at[g, zz])
        copy = remote(
            hbuf.at[g, c], hbuf.at[g, c], f_send.at[g], f_sem.at[g], z * 2 + 1 - c, m
        )
        copy.start()
        forwards.append(copy)

    def multiply(g, cut):
        lhs = hbuf[g].reshape(all_rows, qper * head)
        return jnp.dot(lhs, obuf_w[g, :, cut], preferred_element_type=jnp.float32)

    def gathered(g):
        arrived(hbuf.at[g, 1 - c], f_sem.at[g])
        out_copies[g].wait()

    for g in range(heads_here):
        attention(g)
        if g:
            forward(g - 1)
    forward(heads_here - 1)

    last = heads_here - 1
    pieces = osend.shape[0]
    narrow = width // pieces
    for g in range(last):
        gathered(g)
        for n in range(pieces):
            cut = slice(n * narrow, (n + 1) * narrow)
            if g == 0:
                acc[:, cut] = multiply(g, cut)
            else:
                acc[:, cut] += multiply(g, cut)
    gathered(last)
    zhalf = zs // mp
    out_sends = []
    for n in range(pieces):
        cut = slice(n * narrow, (n + 1) * narrow)
        block_sum = acc[:, cut] + multiply(last, cut)
        for cc in range(2):
            for zz in range(zs):
                first = (cc * zs + zz) * rows
                osend[n, zz // zhalf, zz % zhalf, cc] = block_sum[first:first + rows]
        copy = remote(
            osend.at[n, (m + 1) % mp], orecv.at[n], o_send.at[n], o_sem.at[n], h, (m + 1) % mp
        )
        copy.start()
        out_sends.append(copy)
    for n in range(pieces):
        cut = slice(n * narrow, (n + 1) * narrow)
        out_sends[n].wait_recv()
        out[:, :, :, cut] = (osend[n, m] + orecv[n]).astype(out.dtype)

    for copy, mine in row_sends:
        if mine is None:
            copy.wait_send()
        else:

            @pl.when(jnp.logical_not(mine))
            def _(copy=copy):
                copy.wait_send()

    for copy in ss_sends + stage1 + stage2 + forwards + out_sends:
        copy.wait_send()
    for sends in head_sends:
        for copy in sends:
            copy.wait_send()


def fused(
    stream_rows, norm_gain, query_weight, keyval_weight, output_weight, key_cache, value_cache, lengths
):
    hidden = lax.axis_size("hidden")
    mp = lax.axis_size("mp")
    seqs, steps, narrow = stream_rows.shape
    rows = seqs * steps
    block, heads_here, q_width = query_weight.shape
    head = key_cache.shape[3]
    slots = key_cache.shape[2]
    width = output_weight.shape[2]
    nb = narrow // block
    qper = q_width // head
    chunks = (qper + 2) // 2
    zs = hidden // 2
    all_rows = hidden * rows
    xb = jnp.transpose(stream_rows.reshape(rows, nb, block), (1, 0, 2))
    gain = norm_gain.astype(jnp.float32).reshape(nb, 1, block)
    half = head // 2
    freq = jnp.exp(jnp.arange(half, dtype=jnp.float32) * (-2.0 * math.log(rope_base) / head))
    pos = (lengths[:, None] + jnp.arange(steps, dtype=jnp.int32)[None, :]).astype(jnp.float32)
    angle = pos.reshape(rows, 1) * freq
    cosine = jnp.cos(angle)
    sine = jnp.sin(angle)
    trig = jnp.stack(
        [jnp.concatenate([cosine, cosine], axis=1), jnp.concatenate([-sine, sine], axis=1)]
    )
    lens = jnp.broadcast_to(lengths[:, None, None], (seqs, steps, 128)).reshape(rows, 128)
    f32, bf16, dma = jnp.float32, jnp.bfloat16, pltpu.SemaphoreType.DMA
    pieces = 4
    vmem = pl.BlockSpec(memory_space=pltpu.VMEM)
    hbm = pl.BlockSpec(memory_space=pl.ANY)
    out = pl.pallas_call(
        functools.partial(fused_kernel, hidden=hidden, mp=mp, width=width),
        out_shape=jax.ShapeDtypeStruct((zs // mp, 2, rows, width), bf16),
        in_specs=[vmem] * 4 + [hbm] * 5,
        out_specs=vmem,
        scratch_shapes=[
            pltpu.VMEM((hidden, rows, block), bf16),
            pltpu.VMEM((rows, 128), f32),
            pltpu.VMEM((mp, hidden, rows, 128), f32),
            pltpu.VMEM((1, block), f32),
            pltpu.VMEM((heads_here * all_rows, block * heads_here), bf16),
            pltpu.VMEM((qper + 2, block, heads_here, head), bf16),
            pltpu.VMEM((seqs, heads_here, slots, head), bf16),
            pltpu.VMEM((seqs, heads_here, slots, head), bf16),
            pltpu.VMEM((heads_here, q_width, width), bf16),
            pltpu.VMEM((chunks, 2, zs, heads_here, rows, 2 * head), f32),
            pltpu.VMEM((chunks, zs, heads_here, rows, 2 * head), f32),
            pltpu.VMEM((chunks, zs - 1, heads_here, rows, 2 * head), f32),
            pltpu.VMEM((heads_here, 2, zs, rows, q_width), bf16),
            pltpu.VMEM((all_rows, width), f32),
            pltpu.VMEM((pieces, mp, zs // mp, 2, rows, width // pieces), f32),
            pltpu.VMEM((pieces, zs // mp, 2, rows, width // pieces), f32),
            dma((nb * mp,)),
            dma((hidden,)),
            dma((hidden * mp,)),
            dma((mp, hidden)),
            dma((3,)),
            dma((qper + 2,)),
            dma((2, heads_here)),
            dma((heads_here,)),
            dma((chunks,)),
            dma((chunks,)),
            dma((chunks, zs - 1)),
            dma((chunks, zs - 1)),
            dma((heads_here, zs - 1)),
            dma((heads_here, zs)),
            dma((heads_here,)),
            dma((heads_here,)),
            dma((pieces,)),
            dma((pieces,)),
        ],
        compiler_params=pltpu.CompilerParams(
            collective_id=0, has_side_effects=True, vmem_limit_bytes=60 * 2**20
        ),
        name="fused_decode",
    )(xb, gain, trig, lens, query_weight, keyval_weight, output_weight, key_cache, value_cache)
    return out.reshape(zs // mp * 2 * seqs, steps, width)


def solution(mesh):
    in_specs = (
        P(("groups", "hidden"), None, "mp"),
        P("mp"),
        P("hidden", "mp", None),
        P("hidden", "mp", None),
        P("mp", None, "hidden"),
        P(("groups", "hidden"), "mp", None, None),
        P(("groups", "hidden"), "mp", None, None),
        P(("groups", "hidden")),
    )
    out_specs = P(("groups", "mp"), None, "hidden")
    fits = mesh.shape["hidden"] == 8 and mesh.shape["mp"] == 2
    body = fused if fits else local
    return jax.shard_map(body, mesh=mesh, in_specs=in_specs, out_specs=out_specs, check_vma=False)
```

```python
import functools
import math

import jax
import jax.numpy as jnp
from jax import lax
from jax.experimental import pallas as pl
from jax.experimental.pallas import tpu as pltpu
from jax.sharding import PartitionSpec as P

rope_base = 500000.0


def norm_blocks(pieces, gains, blocks):
    values = pieces.astype(jnp.float32)
    scale = lax.rsqrt(jnp.mean(values * values, axis=(0, 3), keepdims=True) + 1e-05)
    scaled = values * scale * gains.astype(jnp.float32)[:, None, None, :]
    width_parts, seqs, steps_all, narrow = scaled.shape
    whole = jnp.transpose(scaled, (1, 2, 0, 3)).reshape(
        seqs, steps_all, blocks, width_parts * narrow // blocks
    )
    return jnp.transpose(whole, (2, 0, 1, 3)).astype(jnp.bfloat16)


def rotate(values, pos):
    half = values.shape[-1] // 2
    freq = jnp.exp(
        jnp.arange(half, dtype=jnp.float32) * (-2.0 * math.log(rope_base) / values.shape[-1])
    )
    angle = pos[..., None] * freq
    cosine = jnp.cos(angle)
    sine = jnp.sin(angle)
    first = values[..., :half]
    second = values[..., half:]
    return jnp.concatenate(
        [first * cosine - second * sine, second * cosine + first * sine], axis=-1
    )


def attend(query, new_keys, new_vals, key_cache, value_cache, lengths, step, width, count):
    scale = query.shape[-1] ** (-0.5)
    fresh = (
        jnp.einsum("sgqd,stgd->sgqt", query, new_keys, preferred_element_type=jnp.float32) * scale
    )
    keep = jnp.arange(new_keys.shape[1]) <= step
    fresh = jnp.where(keep, fresh, -jnp.inf)

    def block_scores(index):
        scores = (
            jnp.einsum("sgqd,sgkd->sgqk", query, key_cache, preferred_element_type=jnp.float32)
            * scale
        )
        slots = (index * width + jnp.arange(width))[None, :] < lengths[:, None]
        return (scores, slots[:, None, None, :])

    def widen(index, top):
        scores, slots = block_scores(index)
        return jnp.maximum(top, jnp.max(jnp.where(slots, scores, -jnp.inf), axis=-1))

    top = lax.fori_loop(0, count, widen, jnp.max(fresh, axis=-1))
    p_fresh = jnp.where(keep, jnp.exp(fresh - top[..., None]), 0.0)
    total = jnp.sum(p_fresh, axis=-1)
    acc = jnp.einsum(
        "sgqt,stgd->sgqd",
        p_fresh.astype(jnp.bfloat16),
        new_vals,
        preferred_element_type=jnp.float32,
    )

    def accumulate(index, carry):
        acc_now, total_now = carry
        scores, slots = block_scores(index)
        weights = jnp.where(slots, jnp.exp(scores - top[..., None]), 0.0)
        acc_now = acc_now + jnp.einsum(
            "sgqk,sgkd->sgqd",
            weights.astype(jnp.bfloat16),
            value_cache,
            preferred_element_type=jnp.float32,
        )
        return (acc_now, total_now + jnp.sum(weights, axis=-1))

    acc, total = lax.fori_loop(0, count, accumulate, (acc, total))
    return (acc / total[..., None]).astype(jnp.bfloat16)


def local(
    stream_rows,
    norm_gain,
    query_weight,
    keyval_weight,
    output_weight,
    key_cache,
    value_cache,
    lengths,
):
    seqs = stream_rows.shape[0]
    steps_all = stream_rows.shape[1]
    narrow = stream_rows.shape[2]
    pieces, gains = (
        lax.all_gather(stream_rows.reshape(1, seqs, steps_all, narrow), "mp", axis=0, tiled=True),
        lax.all_gather(norm_gain.reshape(1, narrow), "mp", axis=0, tiled=True),
    )
    blocks = lax.axis_size("hidden")
    normed = norm_blocks(pieces, gains, blocks)
    block = query_weight.shape[0]
    groups_here = query_weight.shape[1]
    head = keyval_weight.shape[2] // 2
    per_group = query_weight.shape[2] // head
    q_cols = groups_here * per_group * head
    wq_flat = query_weight.reshape(block, q_cols)
    wkv_flat = keyval_weight.reshape(block, groups_here * 2 * head)
    wo_flat = output_weight.reshape(q_cols, output_weight.shape[2])
    spread = lax.all_to_all(normed, "hidden", split_axis=0, concat_axis=0, tiled=True)
    spread = spread.reshape(blocks * seqs, steps_all, block)
    piece = spread
    flat = piece.reshape(-1, block)
    q_part = jnp.dot(flat, wq_flat, preferred_element_type=jnp.float32)
    kv_part = jnp.dot(flat, wkv_flat, preferred_element_type=jnp.float32)
    joined = jnp.concatenate([q_part, kv_part], axis=1)
    sums = lax.psum_scatter(
        joined.reshape(piece.shape[:-1] + (joined.shape[-1],)),
        "hidden",
        scatter_dimension=0,
        tiled=True,
    )
    qraw = sums[..., :q_cols].reshape(seqs, steps_all, groups_here, per_group, head)
    kvraw = sums[..., q_cols:].reshape(seqs, steps_all, groups_here, 2, head)
    pos = (lengths[:, None] + jnp.arange(steps_all, dtype=jnp.int32)[None, :]).astype(jnp.float32)
    query = rotate(qraw, pos[:, :, None, None]).astype(jnp.bfloat16)
    new_keys = rotate(kvraw[:, :, :, 0, :], pos[:, :, None]).astype(jnp.bfloat16)
    new_vals = kvraw[:, :, :, 1, :].astype(jnp.bfloat16)
    slots_all = key_cache.shape[2]
    count = 1
    results = []
    for step in range(steps_all):
        heads = attend(
            query[:, step],
            new_keys,
            new_vals,
            key_cache,
            value_cache,
            lengths,
            step,
            slots_all,
            count,
        )
        results.append(heads.reshape(seqs, q_cols))
    heads_all = jnp.stack(results, axis=1)
    piece = lax.all_gather(heads_all, "hidden", axis=0, tiled=True)
    flat = piece.reshape(-1, q_cols)
    product = jnp.dot(flat, wo_flat, preferred_element_type=jnp.float32)
    partial_value = product.reshape(piece.shape[:-1] + (wo_flat.shape[1],))
    return lax.psum_scatter(partial_value, "mp", scatter_dimension=0, tiled=True).astype(
        jnp.bfloat16
    )


def fused_kernel(
    stream, gain, trig, wq, wkv, wo, kcache, vcache, out,
    xr, ssl, ssr, xb, xexp, wbuf, kbuf, vbuf, obuf_w, part, recv1, recv2, hbuf, acc, osend, orecv,
    xsend_sem, xsem, ss_sem, wsem, csem, wosem,
    s1_send, s1_sem, s2_send, s2_sem, h_send, h_sem, f_send, f_sem, o_send, o_sem,
    *, hidden, mp, width,
):
    gy = lax.axis_index("groups")
    h = lax.axis_index("hidden")
    m = lax.axis_index("mp")
    z = h // 2
    c = h % 2
    zs = hidden // 2
    nb, rows, block = xb.shape
    heads_here = wq.shape[1]
    head = kcache.shape[3]
    qper = wq.shape[2] // head
    slots = kcache.shape[2]
    chunks = (qper + 2) // 2
    all_rows = hidden * rows
    depth = block * heads_here

    def at(hh, mm):
        return (gy, hh, mm)

    def remote(src, dst, send, recv, hh, mm):
        return pltpu.make_async_remote_copy(
            src_ref=src, dst_ref=dst, send_sem=send, recv_sem=recv,
            device_id=at(hh, mm), device_id_type=pl.DeviceIdType.MESH,
        )

    def arrived(ref, sem):
        pltpu.make_async_copy(ref, ref, sem).wait()

    weight_copies = []
    for j in range(qper + 2):
        if j < 2:
            src = wkv.at[:, :, pl.ds(j * head, head)]
        else:
            src = wq.at[:, :, pl.ds((j - 2) * head, head)]
        copy = pltpu.make_async_copy(src, wbuf.at[j], wsem.at[j])
        copy.start()
        weight_copies.append(copy)

    barrier = pltpu.get_barrier_semaphore()
    for dh in range(hidden):
        for dm in range(mp):
            if dh or dm:
                pl.semaphore_signal(
                    barrier, inc=1, device_id=at((h + dh) % hidden, (m + dm) % mp),
                    device_id_type=pl.DeviceIdType.MESH,
                )
    pl.semaphore_wait(barrier, hidden * mp - 1)

    stream_f = stream[...].astype(jnp.float32)
    values = jnp.concatenate([stream_f[s] for s in range(stream.shape[0])], axis=0)
    squares = jnp.sum(values * values, axis=-1, keepdims=True)
    ssl[...] = jnp.broadcast_to(squares, ssl.shape)
    ss_copy = remote(ssl, ssr, ss_sem.at[0], ss_sem.at[1], h, (m + 1) % mp)
    ss_copy.start()
    ss_copy.wait_recv()
    total_sq = ssl[...] + ssr[...]
    scale = lax.rsqrt(total_sq / (nb * mp * block) + 1e-05)[:, :1]
    normed_here = values * scale * gain[...].astype(jnp.float32)
    for b in range(nb):
        xb[b] = normed_here[:, b * block:(b + 1) * block].astype(jnp.bfloat16)

    row_sends = []
    for b in range(nb):
        for dm in range(mp):
            hh = m * nb + b
            mm = (m + dm) % mp
            copy = remote(
                xb.at[b], xr.at[h], xsend_sem.at[b * mp + dm], xsem.at[h], hh, mm
            )
            if dm == 0:
                mine = hh == h
                local_copy = pltpu.make_async_copy(xb.at[b], xr.at[h], xsem.at[h])

                @pl.when(mine)
                def _(local_copy=local_copy):
                    local_copy.start()

                @pl.when(jnp.logical_not(mine))
                def _(copy=copy):
                    copy.start()

                row_sends.append((copy, mine))
            else:
                copy.start()
                row_sends.append((copy, None))

    cache_copies = []
    for g in range(heads_here):
        pair = (
            pltpu.make_async_copy(kcache.at[:, g], kbuf.at[:, g], csem.at[0, g]),
            pltpu.make_async_copy(vcache.at[:, g], vbuf.at[:, g], csem.at[1, g]),
        )
        for copy in pair:
            copy.start()
        cache_copies.append(pair)
    out_copies = []
    for g in range(heads_here):
        copy = pltpu.make_async_copy(wo.at[g], obuf_w.at[g], wosem.at[g])
        copy.start()
        out_copies.append(copy)

    for src in range(hidden):
        arrived(xr.at[src], xsem.at[src])
    normed = xr[...].astype(jnp.float32).reshape(all_rows, block).astype(jnp.bfloat16)

    lane = 128
    wide = lane * heads_here
    row_of = lax.broadcasted_iota(jnp.int32, (lane, wide), 0)
    col_of = lax.broadcasted_iota(jnp.int32, (lane, wide), 1)
    spread = jnp.where(col_of // heads_here == row_of, 1.0, 0.0).astype(jnp.bfloat16)
    which = lax.broadcasted_iota(jnp.int32, (all_rows, wide), 1) % heads_here
    for i in range(block // lane):
        rep = jnp.dot(
            normed[:, i * lane:(i + 1) * lane], spread, preferred_element_type=jnp.float32
        )
        for g in range(heads_here):
            xexp[g * all_rows:(g + 1) * all_rows, i * wide:(i + 1) * wide] = jnp.where(
                which == g, rep, 0.0
            ).astype(jnp.bfloat16)

    flat_w = wbuf.reshape(qper + 2, depth, head)
    span = min(depth, 2048)
    stage1 = []
    stage2 = []

    def project(ch):
        for j in (2 * ch, 2 * ch + 1):
            weight_copies[j].wait()

        def body(k, total):
            cut = pl.ds(pl.multiple_of(k * span, span), span)
            rhs = jnp.concatenate([flat_w[2 * ch, cut, :], flat_w[2 * ch + 1, cut, :]], axis=1)
            return total + jnp.dot(xexp[:, cut], rhs, preferred_element_type=jnp.float32)

        result = lax.fori_loop(
            0, depth // span, body,
            jnp.zeros((heads_here * all_rows, 2 * head), jnp.float32),
        )
        for g in range(heads_here):
            for hh in range(hidden):
                first = g * all_rows + hh * rows
                part[ch, hh % 2, hh // 2, g] = result[first:first + rows, :]
        copy = remote(
            part.at[ch, 1 - c], recv1.at[ch], s1_send.at[ch], s1_sem.at[ch], z * 2 + 1 - c, m
        )
        copy.start()
        stage1.append(copy)

    def pass_on(ch):
        stage1[ch].wait_recv()
        part[ch, c] = part[ch, c] + recv1[ch]
        for dz in range(1, zs):
            zz = (z + dz) % zs
            copy = remote(
                part.at[ch, c, zz], recv2.at[ch, dz - 1],
                s2_send.at[ch, dz - 1], s2_sem.at[ch, dz - 1], zz * 2 + c, m,
            )
            copy.start()
            stage2.append(copy)

    for ch in range(chunks):
        project(ch)
        if ch:
            pass_on(ch - 1)
    pass_on(chunks - 1)

    cosine = trig[0]
    sine = trig[1]

    def rotated(values):
        return values * cosine + pltpu.roll(values, head // 2, 1) * sine

    for copy in stage2:
        copy.wait_recv()

    def summed(ch, g):
        total = part[ch, c, z, g]
        for dz in range(1, zs):
            total = total + recv2[ch, dz - 1, g]
        return total

    seqs = kcache.shape[0]
    steps = rows // seqs
    many = qper * rows
    row_id = lax.broadcasted_iota(jnp.int32, (many, 1), 0) % rows
    row_seq = row_id // steps
    row_step = row_id % steps
    limit = jnp.concatenate([trig[2]] * qper, axis=0)[:, :1]
    slot_ok = lax.broadcasted_iota(jnp.int32, (many, slots), 1).astype(jnp.float32) < limit
    extra = lax.broadcasted_iota(jnp.int32, (many, head), 1)
    fresh_ok = (extra // steps == row_seq) & (extra % steps <= row_step)
    factor = head ** (-0.5)
    rest = jnp.zeros((head - rows, head), jnp.float32)
    nt = (((1,), (1,)), ((), ()))
    head_sends = []
    forwards = []

    def attention(g):
        kv = summed(0, g)
        new_key = jnp.concatenate([rotated(kv[:, :head]), rest], axis=0).astype(jnp.bfloat16)
        new_val = jnp.concatenate([kv[:, head:], rest], axis=0).astype(jnp.bfloat16)
        queries = []
        for ch in range(1, chunks):
            both = summed(ch, g)
            queries.append(rotated(both[:, :head]))
            queries.append(rotated(both[:, head:]))
        query = jnp.concatenate(queries, axis=0).astype(jnp.bfloat16)
        for copy in cache_copies[g]:
            copy.wait()
        scores = None
        for s in range(seqs):
            one = lax.dot_general(query, kbuf[s, g], nt, preferred_element_type=jnp.float32)
            scores = one if s == 0 else jnp.where(row_seq == s, one, scores)
        scores = jnp.where(slot_ok, scores * factor, -jnp.inf)
        fresh = lax.dot_general(query, new_key, nt, preferred_element_type=jnp.float32)
        fresh = jnp.where(fresh_ok, fresh * factor, -jnp.inf)
        top = jnp.maximum(
            jnp.max(scores, axis=-1, keepdims=True), jnp.max(fresh, axis=-1, keepdims=True)
        )
        p = jnp.exp(scores - top)
        p_fresh = jnp.exp(fresh - top)
        total = jnp.sum(p, axis=-1, keepdims=True) + jnp.sum(p_fresh, axis=-1, keepdims=True)
        weights = p.astype(jnp.bfloat16)
        value = None
        for s in range(seqs):
            one = jnp.dot(weights, vbuf[s, g], preferred_element_type=jnp.float32)
            value = one if s == 0 else jnp.where(row_seq == s, one, value)
        value = value + jnp.dot(
            p_fresh.astype(jnp.bfloat16), new_val, preferred_element_type=jnp.float32
        )
        value = value / total
        line = jnp.concatenate([value[j * rows:(j + 1) * rows] for j in range(qper)], axis=1)
        hbuf[g, c, z] = line.astype(jnp.bfloat16)
        sends = []
        for dz in range(1, zs):
            zz = (z + dz) % zs
            copy = remote(
                hbuf.at[g, c, z], hbuf.at[g, c, z],
                h_send.at[g, dz - 1], h_sem.at[g, z], zz * 2 + c, m,
            )
            copy.start()
            sends.append(copy)
        head_sends.append(sends)

    def forward(g):
        for dz in range(1, zs):
            zz = (z + dz) % zs
            arrived(hbuf.at[g, c, zz], h_sem.at[g, zz])
        copy = remote(
            hbuf.at[g, c], hbuf.at[g, c], f_send.at[g], f_sem.at[g], z * 2 + 1 - c, m
        )
        copy.start()
        forwards.append(copy)

    def multiply(g, cut):
        lhs = hbuf[g].reshape(all_rows, qper * head)
        return jnp.dot(lhs, obuf_w[g, :, cut], preferred_element_type=jnp.float32)

    def gathered(g):
        arrived(hbuf.at[g, 1 - c], f_sem.at[g])
        out_copies[g].wait()

    for g in range(heads_here):
        attention(g)
        if g:
            forward(g - 1)
    forward(heads_here - 1)

    last = heads_here - 1
    pieces = osend.shape[0]
    narrow = width // pieces
    for g in range(last):
        gathered(g)
        for n in range(pieces):
            cut = slice(n * narrow, (n + 1) * narrow)
            if g == 0:
                acc[:, cut] = multiply(g, cut)
            else:
                acc[:, cut] += multiply(g, cut)
    gathered(last)
    zhalf = zs // mp
    out_sends = []
    for n in range(pieces):
        cut = slice(n * narrow, (n + 1) * narrow)
        block_sum = acc[:, cut] + multiply(last, cut)
        for cc in range(2):
            for zz in range(zs):
                first = (cc * zs + zz) * rows
                osend[n, zz // zhalf, zz % zhalf, cc] = block_sum[first:first + rows]
        copy = remote(
            osend.at[n, (m + 1) % mp], orecv.at[n], o_send.at[n], o_sem.at[n], h, (m + 1) % mp
        )
        copy.start()
        out_sends.append(copy)
    for n in range(pieces):
        cut = slice(n * narrow, (n + 1) * narrow)
        out_sends[n].wait_recv()
        out[:, :, :, cut] = (osend[n, m] + orecv[n]).astype(out.dtype)

    for copy, mine in row_sends:
        if mine is None:
            copy.wait_send()
        else:

            @pl.when(jnp.logical_not(mine))
            def _(copy=copy):
                copy.wait_send()

    for copy in [ss_copy] + stage1 + stage2 + forwards + out_sends:
        copy.wait_send()
    for sends in head_sends:
        for copy in sends:
            copy.wait_send()


def fused(
    stream_rows, norm_gain, query_weight, keyval_weight, output_weight, key_cache, value_cache, lengths
):
    hidden = lax.axis_size("hidden")
    mp = lax.axis_size("mp")
    seqs, steps, narrow = stream_rows.shape
    rows = seqs * steps
    block, heads_here, q_width = query_weight.shape
    head = key_cache.shape[3]
    slots = key_cache.shape[2]
    width = output_weight.shape[2]
    nb = narrow // block
    qper = q_width // head
    chunks = (qper + 2) // 2
    zs = hidden // 2
    all_rows = hidden * rows
    gain = norm_gain.reshape(1, narrow)
    half = head // 2
    freq = jnp.exp(jnp.arange(half, dtype=jnp.float32) * (-2.0 * math.log(rope_base) / head))
    filled = jnp.broadcast_to(lengths[:, None], (seqs, steps)).reshape(rows, 1)
    step_of = jnp.arange(rows, dtype=jnp.int32)[:, None] % steps
    angle = (filled + step_of).astype(jnp.float32) * jnp.concatenate([freq, freq])
    sign = jnp.where(jnp.arange(head) < half, -1.0, 1.0)
    kind = jnp.arange(3)[:, None, None]
    trig = jnp.where(
        kind == 0, jnp.cos(angle),
        jnp.where(kind == 1, sign * jnp.sin(angle), filled.astype(jnp.float32)),
    )
    f32, bf16, dma = jnp.float32, jnp.bfloat16, pltpu.SemaphoreType.DMA
    pieces = 4
    vmem = pl.BlockSpec(memory_space=pltpu.VMEM)
    hbm = pl.BlockSpec(memory_space=pl.ANY)
    out = pl.pallas_call(
        functools.partial(fused_kernel, hidden=hidden, mp=mp, width=width),
        out_shape=jax.ShapeDtypeStruct((zs // mp, 2, rows, width), bf16),
        in_specs=[vmem] * 3 + [hbm] * 5,
        out_specs=vmem,
        scratch_shapes=[
            pltpu.VMEM((hidden, rows, block), bf16),
            pltpu.VMEM((rows, 128), f32),
            pltpu.VMEM((rows, 128), f32),
            pltpu.VMEM((nb, rows, block), bf16),
            pltpu.VMEM((heads_here * all_rows, block * heads_here), bf16),
            pltpu.VMEM((qper + 2, block, heads_here, head), bf16),
            pltpu.VMEM((seqs, heads_here, slots, head), bf16),
            pltpu.VMEM((seqs, heads_here, slots, head), bf16),
            pltpu.VMEM((heads_here, q_width, width), bf16),
            pltpu.VMEM((chunks, 2, zs, heads_here, rows, 2 * head), f32),
            pltpu.VMEM((chunks, zs, heads_here, rows, 2 * head), f32),
            pltpu.VMEM((chunks, zs - 1, heads_here, rows, 2 * head), f32),
            pltpu.VMEM((heads_here, 2, zs, rows, q_width), bf16),
            pltpu.VMEM((all_rows, width), f32),
            pltpu.VMEM((pieces, mp, zs // mp, 2, rows, width // pieces), f32),
            pltpu.VMEM((pieces, zs // mp, 2, rows, width // pieces), f32),
            dma((nb * mp,)),
            dma((hidden,)),
            dma((2,)),
            dma((qper + 2,)),
            dma((2, heads_here)),
            dma((heads_here,)),
            dma((chunks,)),
            dma((chunks,)),
            dma((chunks, zs - 1)),
            dma((chunks, zs - 1)),
            dma((heads_here, zs - 1)),
            dma((heads_here, zs)),
            dma((heads_here,)),
            dma((heads_here,)),
            dma((pieces,)),
            dma((pieces,)),
        ],
        compiler_params=pltpu.CompilerParams(
            collective_id=0, has_side_effects=True, vmem_limit_bytes=60 * 2**20
        ),
        name="fused_decode",
    )(stream_rows, gain, trig, query_weight, keyval_weight, output_weight, key_cache, value_cache)
    return out.reshape(zs // mp * 2 * seqs, steps, width)


def solution(mesh):
    in_specs = (
        P(("groups", "hidden"), None, "mp"),
        P("mp"),
        P("hidden", "mp", None),
        P("hidden", "mp", None),
        P("mp", None, "hidden"),
        P(("groups", "hidden"), "mp", None, None),
        P(("groups", "hidden"), "mp", None, None),
        P(("groups", "hidden")),
    )
    out_specs = P(("groups", "mp"), None, "hidden")
    fits = mesh.shape["hidden"] == 8 and mesh.shape["mp"] == 2
    body = fused if fits else local
    return jax.shard_map(body, mesh=mesh, in_specs=in_specs, out_specs=out_specs, check_vma=False)
```

```python
import functools
import math

import jax
import jax.numpy as jnp
from jax import lax
from jax.experimental import pallas as pl
from jax.experimental.pallas import tpu as pltpu
from jax.sharding import PartitionSpec as P

rope_base = 500000.0


def norm_blocks(pieces, gains, blocks):
    values = pieces.astype(jnp.float32)
    scale = lax.rsqrt(jnp.mean(values * values, axis=(0, 3), keepdims=True) + 1e-05)
    scaled = values * scale * gains.astype(jnp.float32)[:, None, None, :]
    width_parts, seqs, steps_all, narrow = scaled.shape
    whole = jnp.transpose(scaled, (1, 2, 0, 3)).reshape(
        seqs, steps_all, blocks, width_parts * narrow // blocks
    )
    return jnp.transpose(whole, (2, 0, 1, 3)).astype(jnp.bfloat16)


def rotate(values, pos):
    half = values.shape[-1] // 2
    freq = jnp.exp(
        jnp.arange(half, dtype=jnp.float32) * (-2.0 * math.log(rope_base) / values.shape[-1])
    )
    angle = pos[..., None] * freq
    cosine = jnp.cos(angle)
    sine = jnp.sin(angle)
    first = values[..., :half]
    second = values[..., half:]
    return jnp.concatenate(
        [first * cosine - second * sine, second * cosine + first * sine], axis=-1
    )


def attend(query, new_keys, new_vals, key_cache, value_cache, lengths, step, width, count):
    scale = query.shape[-1] ** (-0.5)
    fresh = (
        jnp.einsum("sgqd,stgd->sgqt", query, new_keys, preferred_element_type=jnp.float32) * scale
    )
    keep = jnp.arange(new_keys.shape[1]) <= step
    fresh = jnp.where(keep, fresh, -jnp.inf)

    def block_scores(index):
        scores = (
            jnp.einsum("sgqd,sgkd->sgqk", query, key_cache, preferred_element_type=jnp.float32)
            * scale
        )
        slots = (index * width + jnp.arange(width))[None, :] < lengths[:, None]
        return (scores, slots[:, None, None, :])

    def widen(index, top):
        scores, slots = block_scores(index)
        return jnp.maximum(top, jnp.max(jnp.where(slots, scores, -jnp.inf), axis=-1))

    top = lax.fori_loop(0, count, widen, jnp.max(fresh, axis=-1))
    p_fresh = jnp.where(keep, jnp.exp(fresh - top[..., None]), 0.0)
    total = jnp.sum(p_fresh, axis=-1)
    acc = jnp.einsum(
        "sgqt,stgd->sgqd",
        p_fresh.astype(jnp.bfloat16),
        new_vals,
        preferred_element_type=jnp.float32,
    )

    def accumulate(index, carry):
        acc_now, total_now = carry
        scores, slots = block_scores(index)
        weights = jnp.where(slots, jnp.exp(scores - top[..., None]), 0.0)
        acc_now = acc_now + jnp.einsum(
            "sgqk,sgkd->sgqd",
            weights.astype(jnp.bfloat16),
            value_cache,
            preferred_element_type=jnp.float32,
        )
        return (acc_now, total_now + jnp.sum(weights, axis=-1))

    acc, total = lax.fori_loop(0, count, accumulate, (acc, total))
    return (acc / total[..., None]).astype(jnp.bfloat16)


def local(
    stream_rows,
    norm_gain,
    query_weight,
    keyval_weight,
    output_weight,
    key_cache,
    value_cache,
    lengths,
):
    seqs = stream_rows.shape[0]
    steps_all = stream_rows.shape[1]
    narrow = stream_rows.shape[2]
    pieces, gains = (
        lax.all_gather(stream_rows.reshape(1, seqs, steps_all, narrow), "mp", axis=0, tiled=True),
        lax.all_gather(norm_gain.reshape(1, narrow), "mp", axis=0, tiled=True),
    )
    blocks = lax.axis_size("hidden")
    normed = norm_blocks(pieces, gains, blocks)
    block = query_weight.shape[0]
    groups_here = query_weight.shape[1]
    head = keyval_weight.shape[2] // 2
    per_group = query_weight.shape[2] // head
    q_cols = groups_here * per_group * head
    wq_flat = query_weight.reshape(block, q_cols)
    wkv_flat = keyval_weight.reshape(block, groups_here * 2 * head)
    wo_flat = output_weight.reshape(q_cols, output_weight.shape[2])
    spread = lax.all_to_all(normed, "hidden", split_axis=0, concat_axis=0, tiled=True)
    spread = spread.reshape(blocks * seqs, steps_all, block)
    piece = spread
    flat = piece.reshape(-1, block)
    q_part = jnp.dot(flat, wq_flat, preferred_element_type=jnp.float32)
    kv_part = jnp.dot(flat, wkv_flat, preferred_element_type=jnp.float32)
    joined = jnp.concatenate([q_part, kv_part], axis=1)
    sums = lax.psum_scatter(
        joined.reshape(piece.shape[:-1] + (joined.shape[-1],)),
        "hidden",
        scatter_dimension=0,
        tiled=True,
    )
    qraw = sums[..., :q_cols].reshape(seqs, steps_all, groups_here, per_group, head)
    kvraw = sums[..., q_cols:].reshape(seqs, steps_all, groups_here, 2, head)
    pos = (lengths[:, None] + jnp.arange(steps_all, dtype=jnp.int32)[None, :]).astype(jnp.float32)
    query = rotate(qraw, pos[:, :, None, None]).astype(jnp.bfloat16)
    new_keys = rotate(kvraw[:, :, :, 0, :], pos[:, :, None]).astype(jnp.bfloat16)
    new_vals = kvraw[:, :, :, 1, :].astype(jnp.bfloat16)
    slots_all = key_cache.shape[2]
    count = 1
    results = []
    for step in range(steps_all):
        heads = attend(
            query[:, step],
            new_keys,
            new_vals,
            key_cache,
            value_cache,
            lengths,
            step,
            slots_all,
            count,
        )
        results.append(heads.reshape(seqs, q_cols))
    heads_all = jnp.stack(results, axis=1)
    piece = lax.all_gather(heads_all, "hidden", axis=0, tiled=True)
    flat = piece.reshape(-1, q_cols)
    product = jnp.dot(flat, wo_flat, preferred_element_type=jnp.float32)
    partial_value = product.reshape(piece.shape[:-1] + (wo_flat.shape[1],))
    return lax.psum_scatter(partial_value, "mp", scatter_dimension=0, tiled=True).astype(
        jnp.bfloat16
    )


def fused_kernel(
    stream, gain, trig, wq, wkv, wo, kcache, vcache, out,
    xr, ssl, ssr, xb, xexp, wbuf, kbuf, vbuf, obuf_w, part, recv1, recv2, hbuf, acc, osend, olink, orecv,
    xsend_sem, xsem, ss_sem, wsem, csem, wosem,
    s1_send, s1_sem, s2_send, s2_sem, h_send, h_sem, f_send, f_sem, o_send, o_sem,
    *, hidden, mp, width,
):
    gy = lax.axis_index("groups")
    h = lax.axis_index("hidden")
    m = lax.axis_index("mp")
    z = h // 2
    c = h % 2
    zs = hidden // 2
    nb, rows, block = xb.shape
    heads_here = wq.shape[1]
    head = kcache.shape[3]
    qper = wq.shape[2] // head
    slots = kcache.shape[2]
    chunks = (qper + 2) // 2
    all_rows = hidden * rows
    depth = block * heads_here

    def at(hh, mm):
        return (gy, hh, mm)

    def remote(src, dst, send, recv, hh, mm):
        return pltpu.make_async_remote_copy(
            src_ref=src, dst_ref=dst, send_sem=send, recv_sem=recv,
            device_id=at(hh, mm), device_id_type=pl.DeviceIdType.MESH,
        )

    def arrived(ref, sem):
        pltpu.make_async_copy(ref, ref, sem).wait()

    weight_copies = []
    for j in range(qper + 2):
        if j < 2:
            src = wkv.at[:, :, pl.ds(j * head, head)]
        else:
            src = wq.at[:, :, pl.ds((j - 2) * head, head)]
        copy = pltpu.make_async_copy(src, wbuf.at[j], wsem.at[j])
        copy.start()
        weight_copies.append(copy)

    barrier = pltpu.get_barrier_semaphore()
    for dh in range(hidden):
        for dm in range(mp):
            if dh or dm:
                pl.semaphore_signal(
                    barrier, inc=1, device_id=at((h + dh) % hidden, (m + dm) % mp),
                    device_id_type=pl.DeviceIdType.MESH,
                )
    pl.semaphore_wait(barrier, hidden * mp - 1)

    stream_f = stream[...].astype(jnp.float32)
    values = jnp.concatenate([stream_f[s] for s in range(stream.shape[0])], axis=0)
    squares = jnp.sum(values * values, axis=-1, keepdims=True)
    ssl[...] = jnp.broadcast_to(squares, ssl.shape)
    ss_copy = remote(ssl, ssr, ss_sem.at[0], ss_sem.at[1], h, (m + 1) % mp)
    ss_copy.start()
    ss_copy.wait_recv()
    total_sq = ssl[...] + ssr[...]
    scale = lax.rsqrt(total_sq / (nb * mp * block) + 1e-05)[:, :1]
    normed_here = values * scale * gain[...].astype(jnp.float32)
    for b in range(nb):
        xb[b] = normed_here[:, b * block:(b + 1) * block].astype(jnp.bfloat16)

    row_sends = []
    for b in range(nb):
        for dm in range(mp):
            hh = m * nb + b
            mm = (m + dm) % mp
            copy = remote(
                xb.at[b], xr.at[h], xsend_sem.at[b * mp + dm], xsem.at[h], hh, mm
            )
            if dm == 0:
                mine = hh == h
                local_copy = pltpu.make_async_copy(xb.at[b], xr.at[h], xsem.at[h])

                @pl.when(mine)
                def _(local_copy=local_copy):
                    local_copy.start()

                @pl.when(jnp.logical_not(mine))
                def _(copy=copy):
                    copy.start()

                row_sends.append((copy, mine))
            else:
                copy.start()
                row_sends.append((copy, None))

    cache_copies = []
    for g in range(heads_here):
        pair = (
            pltpu.make_async_copy(kcache.at[:, g], kbuf.at[:, g], csem.at[0, g]),
            pltpu.make_async_copy(vcache.at[:, g], vbuf.at[:, g], csem.at[1, g]),
        )
        for copy in pair:
            copy.start()
        cache_copies.append(pair)
    out_copies = []
    for g in range(heads_here):
        copy = pltpu.make_async_copy(wo.at[g], obuf_w.at[g], wosem.at[g])
        copy.start()
        out_copies.append(copy)

    for src in range(hidden):
        arrived(xr.at[src], xsem.at[src])
    normed = xr[...].astype(jnp.float32).reshape(all_rows, block).astype(jnp.bfloat16)

    lane = 128
    wide = lane * heads_here
    row_of = lax.broadcasted_iota(jnp.int32, (lane, wide), 0)
    col_of = lax.broadcasted_iota(jnp.int32, (lane, wide), 1)
    spread = jnp.where(col_of // heads_here == row_of, 1.0, 0.0).astype(jnp.bfloat16)
    which = lax.broadcasted_iota(jnp.int32, (all_rows, wide), 1) % heads_here
    for i in range(block // lane):
        rep = jnp.dot(
            normed[:, i * lane:(i + 1) * lane], spread, preferred_element_type=jnp.float32
        )
        for g in range(heads_here):
            xexp[g * all_rows:(g + 1) * all_rows, i * wide:(i + 1) * wide] = jnp.where(
                which == g, rep, 0.0
            ).astype(jnp.bfloat16)

    flat_w = wbuf.reshape(qper + 2, depth, head)
    span = min(depth, 2048)
    stage1 = []
    stage2 = []

    def project(ch):
        for j in (2 * ch, 2 * ch + 1):
            weight_copies[j].wait()

        def body(k, total):
            cut = pl.ds(pl.multiple_of(k * span, span), span)
            rhs = jnp.concatenate([flat_w[2 * ch, cut, :], flat_w[2 * ch + 1, cut, :]], axis=1)
            return total + jnp.dot(xexp[:, cut], rhs, preferred_element_type=jnp.float32)

        result = lax.fori_loop(
            0, depth // span, body,
            jnp.zeros((heads_here * all_rows, 2 * head), jnp.float32),
        )
        for g in range(heads_here):
            for hh in range(hidden):
                first = g * all_rows + hh * rows
                part[ch, hh % 2, hh // 2, g] = result[first:first + rows, :]
        copy = remote(
            part.at[ch, 1 - c], recv1.at[ch], s1_send.at[ch], s1_sem.at[ch], z * 2 + 1 - c, m
        )
        copy.start()
        stage1.append(copy)

    def pass_on(ch):
        stage1[ch].wait_recv()
        part[ch, c] = part[ch, c] + recv1[ch]
        for dz in range(1, zs):
            zz = (z + dz) % zs
            copy = remote(
                part.at[ch, c, zz], recv2.at[ch, dz - 1],
                s2_send.at[ch, dz - 1], s2_sem.at[ch, dz - 1], zz * 2 + c, m,
            )
            copy.start()
            stage2.append(copy)

    for ch in range(chunks):
        project(ch)
        if ch:
            pass_on(ch - 1)
    pass_on(chunks - 1)

    cosine = trig[0]
    sine = trig[1]

    def rotated(values):
        return values * cosine + pltpu.roll(values, head // 2, 1) * sine

    for copy in stage2:
        copy.wait_recv()

    def summed(ch, g):
        total = part[ch, c, z, g]
        for dz in range(1, zs):
            total = total + recv2[ch, dz - 1, g]
        return total

    seqs = kcache.shape[0]
    steps = rows // seqs
    many = qper * rows
    row_id = lax.broadcasted_iota(jnp.int32, (many, 1), 0) % rows
    row_seq = row_id // steps
    row_step = row_id % steps
    limit = jnp.concatenate([trig[2]] * qper, axis=0)[:, :1]
    slot_ok = lax.broadcasted_iota(jnp.int32, (many, slots), 1).astype(jnp.float32) < limit
    extra = lax.broadcasted_iota(jnp.int32, (many, head), 1)
    fresh_ok = (extra // steps == row_seq) & (extra % steps <= row_step)
    factor = head ** (-0.5)
    rest = jnp.zeros((head - rows, head), jnp.float32)
    nt = (((1,), (1,)), ((), ()))
    head_sends = []
    forwards = []

    def attention(g):
        kv = summed(0, g)
        new_key = jnp.concatenate([rotated(kv[:, :head]), rest], axis=0).astype(jnp.bfloat16)
        new_val = jnp.concatenate([kv[:, head:], rest], axis=0).astype(jnp.bfloat16)
        queries = []
        for ch in range(1, chunks):
            both = summed(ch, g)
            queries.append(rotated(both[:, :head]))
            queries.append(rotated(both[:, head:]))
        query = jnp.concatenate(queries, axis=0).astype(jnp.bfloat16)
        for copy in cache_copies[g]:
            copy.wait()
        scores = None
        for s in range(seqs):
            one = lax.dot_general(query, kbuf[s, g], nt, preferred_element_type=jnp.float32)
            scores = one if s == 0 else jnp.where(row_seq == s, one, scores)
        scores = jnp.where(slot_ok, scores * factor, -jnp.inf)
        fresh = lax.dot_general(query, new_key, nt, preferred_element_type=jnp.float32)
        fresh = jnp.where(fresh_ok, fresh * factor, -jnp.inf)
        top = jnp.maximum(
            jnp.max(scores, axis=-1, keepdims=True), jnp.max(fresh, axis=-1, keepdims=True)
        )
        p = jnp.exp(scores - top)
        p_fresh = jnp.exp(fresh - top)
        total = jnp.sum(p, axis=-1, keepdims=True) + jnp.sum(p_fresh, axis=-1, keepdims=True)
        weights = p.astype(jnp.bfloat16)
        value = None
        for s in range(seqs):
            one = jnp.dot(weights, vbuf[s, g], preferred_element_type=jnp.float32)
            value = one if s == 0 else jnp.where(row_seq == s, one, value)
        value = value + jnp.dot(
            p_fresh.astype(jnp.bfloat16), new_val, preferred_element_type=jnp.float32
        )
        value = value / total
        line = jnp.concatenate([value[j * rows:(j + 1) * rows] for j in range(qper)], axis=1)
        hbuf[g, c, z] = line.astype(jnp.bfloat16)
        sends = []
        for dz in range(1, zs):
            zz = (z + dz) % zs
            copy = remote(
                hbuf.at[g, c, z], hbuf.at[g, c, z],
                h_send.at[g, dz - 1], h_sem.at[g, z], zz * 2 + c, m,
            )
            copy.start()
            sends.append(copy)
        head_sends.append(sends)

    def forward(g):
        for dz in range(1, zs):
            zz = (z + dz) % zs
            arrived(hbuf.at[g, c, zz], h_sem.at[g, zz])
        copy = remote(
            hbuf.at[g, c], hbuf.at[g, c], f_send.at[g], f_sem.at[g], z * 2 + 1 - c, m
        )
        copy.start()
        forwards.append(copy)

    def multiply(g, cut):
        lhs = hbuf[g].reshape(all_rows, qper * head)
        return jnp.dot(lhs, obuf_w[g, :, cut], preferred_element_type=jnp.float32)

    def gathered(g):
        arrived(hbuf.at[g, 1 - c], f_sem.at[g])
        out_copies[g].wait()

    for g in range(heads_here):
        attention(g)
        if g:
            forward(g - 1)
    forward(heads_here - 1)

    last = heads_here - 1
    pieces = osend.shape[0]
    narrow = width // pieces
    for g in range(last):
        gathered(g)
        for n in range(pieces):
            cut = slice(n * narrow, (n + 1) * narrow)
            if g == 0:
                acc[:, cut] = multiply(g, cut)
            else:
                acc[:, cut] += multiply(g, cut)
    gathered(last)
    zhalf = zs // mp
    out_sends = []
    for n in range(pieces):
        cut = slice(n * narrow, (n + 1) * narrow)
        block_sum = acc[:, cut] + multiply(last, cut)
        for cc in range(2):
            for zz in range(zs):
                first = (cc * zs + zz) * rows
                osend[n, zz // zhalf, zz % zhalf, cc] = block_sum[first:first + rows]
                olink[n, zz // zhalf, zz % zhalf, cc] = block_sum[first:first + rows].astype(olink.dtype)
        copy = remote(
            olink.at[n, (m + 1) % mp], orecv.at[n], o_send.at[n], o_sem.at[n], h, (m + 1) % mp
        )
        copy.start()
        out_sends.append(copy)
    for n in range(pieces):
        cut = slice(n * narrow, (n + 1) * narrow)
        out_sends[n].wait_recv()
        out[:, :, :, cut] = (osend[n, m] + orecv[n].astype(jnp.float32)).astype(out.dtype)

    for copy, mine in row_sends:
        if mine is None:
            copy.wait_send()
        else:

            @pl.when(jnp.logical_not(mine))
            def _(copy=copy):
                copy.wait_send()

    for copy in [ss_copy] + stage1 + stage2 + forwards + out_sends:
        copy.wait_send()
    for sends in head_sends:
        for copy in sends:
            copy.wait_send()


def fused(
    stream_rows, norm_gain, query_weight, keyval_weight, output_weight, key_cache, value_cache, lengths
):
    hidden = lax.axis_size("hidden")
    mp = lax.axis_size("mp")
    seqs, steps, narrow = stream_rows.shape
    rows = seqs * steps
    block, heads_here, q_width = query_weight.shape
    head = key_cache.shape[3]
    slots = key_cache.shape[2]
    width = output_weight.shape[2]
    nb = narrow // block
    qper = q_width // head
    chunks = (qper + 2) // 2
    zs = hidden // 2
    all_rows = hidden * rows
    gain = norm_gain.reshape(1, narrow)
    half = head // 2
    freq = jnp.exp(jnp.arange(half, dtype=jnp.float32) * (-2.0 * math.log(rope_base) / head))
    filled = jnp.broadcast_to(lengths[:, None], (seqs, steps)).reshape(rows, 1)
    step_of = jnp.arange(rows, dtype=jnp.int32)[:, None] % steps
    angle = (filled + step_of).astype(jnp.float32) * jnp.concatenate([freq, freq])
    sign = jnp.where(jnp.arange(head) < half, -1.0, 1.0)
    kind = jnp.arange(3)[:, None, None]
    trig = jnp.where(
        kind == 0, jnp.cos(angle),
        jnp.where(kind == 1, sign * jnp.sin(angle), filled.astype(jnp.float32)),
    )
    f32, bf16, dma = jnp.float32, jnp.bfloat16, pltpu.SemaphoreType.DMA
    pieces = 4
    vmem = pl.BlockSpec(memory_space=pltpu.VMEM)
    hbm = pl.BlockSpec(memory_space=pl.ANY)
    out = pl.pallas_call(
        functools.partial(fused_kernel, hidden=hidden, mp=mp, width=width),
        out_shape=jax.ShapeDtypeStruct((zs // mp, 2, rows, width), bf16),
        in_specs=[vmem] * 3 + [hbm] * 5,
        out_specs=vmem,
        scratch_shapes=[
            pltpu.VMEM((hidden, rows, block), bf16),
            pltpu.VMEM((rows, 128), f32),
            pltpu.VMEM((rows, 128), f32),
            pltpu.VMEM((nb, rows, block), bf16),
            pltpu.VMEM((heads_here * all_rows, block * heads_here), bf16),
            pltpu.VMEM((qper + 2, block, heads_here, head), bf16),
            pltpu.VMEM((seqs, heads_here, slots, head), bf16),
            pltpu.VMEM((seqs, heads_here, slots, head), bf16),
            pltpu.VMEM((heads_here, q_width, width), bf16),
            pltpu.VMEM((chunks, 2, zs, heads_here, rows, 2 * head), f32),
            pltpu.VMEM((chunks, zs, heads_here, rows, 2 * head), f32),
            pltpu.VMEM((chunks, zs - 1, heads_here, rows, 2 * head), f32),
            pltpu.VMEM((heads_here, 2, zs, rows, q_width), bf16),
            pltpu.VMEM((all_rows, width), f32),
            pltpu.VMEM((pieces, mp, zs // mp, 2, rows, width // pieces), f32),
            pltpu.VMEM((pieces, mp, zs // mp, 2, rows, width // pieces), bf16),
            pltpu.VMEM((pieces, zs // mp, 2, rows, width // pieces), bf16),
            dma((nb * mp,)),
            dma((hidden,)),
            dma((2,)),
            dma((qper + 2,)),
            dma((2, heads_here)),
            dma((heads_here,)),
            dma((chunks,)),
            dma((chunks,)),
            dma((chunks, zs - 1)),
            dma((chunks, zs - 1)),
            dma((heads_here, zs - 1)),
            dma((heads_here, zs)),
            dma((heads_here,)),
            dma((heads_here,)),
            dma((pieces,)),
            dma((pieces,)),
        ],
        compiler_params=pltpu.CompilerParams(
            collective_id=0, has_side_effects=True, vmem_limit_bytes=60 * 2**20
        ),
        name="fused_decode",
    )(stream_rows, gain, trig, query_weight, keyval_weight, output_weight, key_cache, value_cache)
    return out.reshape(zs // mp * 2 * seqs, steps, width)


def solution(mesh):
    in_specs = (
        P(("groups", "hidden"), None, "mp"),
        P("mp"),
        P("hidden", "mp", None),
        P("hidden", "mp", None),
        P("mp", None, "hidden"),
        P(("groups", "hidden"), "mp", None, None),
        P(("groups", "hidden"), "mp", None, None),
        P(("groups", "hidden")),
    )
    out_specs = P(("groups", "mp"), None, "hidden")
    fits = mesh.shape["hidden"] == 8 and mesh.shape["mp"] == 2
    body = fused if fits else local
    return jax.shard_map(body, mesh=mesh, in_specs=in_specs, out_specs=out_specs, check_vma=False)
```
